32 devices in a mesh: row: 2 (over x), col: 4 (over z), head: 4 (over y, core).
Axes of the slice: x: 2, y: 2, z: 4, core: 2. Of those that a mesh axis runs over, the one named last changes fastest.
Arguments:
- queries: bfloat16 [4, 32, 80, 1024], P('head', None, 'row', 'col'), may hold values from -6.5 to 6.5
- key_vectors: bfloat16 [4, 32, 80, 1024], P('head', None, 'row', 'col'), may hold values from -6.5 to 6.5
- value_vectors: bfloat16 [4, 32, 80, 1024], P('head', None, 'row', 'col'), may hold values from -6 to 6
- gate_logits: bfloat16 [4, 32, 80, 1024], P('head', None, 'row', 'col'), may hold values from -6 to 6
- cotangent: bfloat16 [4, 32, 80, 1024], P('head', None, 'row', 'col'), may hold values from -24 to 24
- pair_normed: bfloat16 [128, 1024, 1024], P('head', 'row', 'col'), may hold values from -6 to 6
- bias_weight: bfloat16 [128, 4], P('head'), may hold values from -0.75 to 0.75
- chain_lengths: int32 [8], replicated, may hold values from 51 to 128, as said below
Outputs:
- query_grad: bfloat16 [4, 32, 80, 1024], P('head', None, 'row', 'col')
- key_grad: bfloat16 [4, 32, 80, 1024], P('head', None, 'row', 'col')
- value_grad: bfloat16 [4, 32, 80, 1024], P('head', None, 'row', 'col')
- gate_grad: bfloat16 [4, 32, 80, 1024], P('head', None, 'row', 'col')
- pair_grad: bfloat16 [128, 1024, 1024], P('head', 'row', 'col')
The draws below stay inside these ranges and needn't reach their ends.
Inputs may be any that keep to these rules, and one draw needn't show every extreme that they name: `chain_lengths`: every chain has at least one token; positions from the sum of the lengths on are padding.
All inputs are finite; a program needn't handle non-finite values.
Results may differ from the reference program's by a relative error of at most 0.027.
Values may be sent and summed in bfloat16 or wider, within the bound.
A program may use at most 128 MiB of HBM per device.

```python
import jax
import jax.numpy as jnp
from jax import lax

PAIR = 128
HEADS = 4
HEAD_DIM = 32
TOKENS = 1024
CHAINS = 8
ROWS = 80


def draw_queries(key, part):
    key = jax.random.fold_in(key, 11)
    values = jax.random.truncated_normal(key, -4.0, 4.0, (HEADS, HEAD_DIM, ROWS, TOKENS), jnp.float32)
    return values.astype(jnp.bfloat16)


def draw_key_vectors(key, part):
    key = jax.random.fold_in(key, 13)
    values = jax.random.truncated_normal(key, -4.0, 4.0, (HEADS, HEAD_DIM, ROWS, TOKENS), jnp.float32)
    return values.astype(jnp.bfloat16)


def draw_chain_lengths(key, part):
    key = jax.random.fold_in(key, 5)
    lengths = jax.random.randint(key, (CHAINS,), TOKENS // 20 + 1, TOKENS // 8, jnp.int32)
    order = jax.random.permutation(jax.random.fold_in(key, 1), CHAINS)
    lengths = lengths.at[order[0]].set(TOKENS // 8)
    lengths = lengths.at[order[1]].set(TOKENS // 20)
    return lengths


def steps_of(rng, extent, pieces, least, high):
    def one(dim, blocks):
        draws = jax.random.uniform(jax.random.fold_in(jax.random.fold_in(rng, 6), dim), (blocks,), jnp.float32, least / len(pieces), high / len(pieces))
        return jnp.repeat(jnp.exp(draws), extent[dim] // blocks).reshape((-1,) + (1,) * (len(extent) - dim - 1))

    loudness = one(*pieces[0])
    for cut in pieces[1:]:
        loudness = loudness * one(*cut)
    return loudness


def scatter_about(stream_key, shape, deviation, bound, cuts=(), kind=jnp.bfloat16):
    factor_of = steps_of(stream_key, shape, cuts, -0.22, 0.18) if cuts else 1.0
    result = jax.random.normal(stream_key, shape, jnp.float32) * deviation * factor_of
    return jnp.minimum(jnp.maximum(result, -bound), bound).astype(kind)


def setup_inputs(seed: int = 0) -> dict:
    arg_keys = jax.random.split(jax.random.key(seed), 9)
    return {
        "queries": draw_queries(jax.random.fold_in(arg_keys[8], 71), 0),
        "key_vectors": draw_key_vectors(jax.random.fold_in(arg_keys[8], 71), 0),
        "value_vectors": scatter_about(arg_keys[2], (HEADS, HEAD_DIM, ROWS, TOKENS), 1.0, 6.0, ((0, 4), (2, 2), (3, 4))),
        "gate_logits": scatter_about(arg_keys[3], (HEADS, HEAD_DIM, ROWS, TOKENS), 1.5, 6.0, ((0, 4), (2, 2), (3, 4))),
        "cotangent": scatter_about(arg_keys[4], (HEADS, HEAD_DIM, ROWS, TOKENS), 4.0, 24.0, ((0, 4), (2, 2), (3, 4))),
        "pair_normed": scatter_about(arg_keys[5], (PAIR, TOKENS, TOKENS), 1.0, 6.0, ((0, 4), (1, 2), (2, 4))),
        "bias_weight": scatter_about(arg_keys[6], (PAIR, HEADS), (PAIR // 2) ** -0.5, 0.75, ((0, 4),)),
        "chain_lengths": draw_chain_lengths(jax.random.fold_in(arg_keys[8], 71), 0),
    }


def round_bf16(source):
    return lax.optimization_barrier(source.astype(jnp.bfloat16)).astype(jnp.float32)


def reference(queries, key_vectors, value_vectors, gate_logits, cotangent, pair_normed, bias_weight, chain_lengths):
    score_scale = HEAD_DIM ** -0.5
    flat_pair = pair_normed.reshape(PAIR, TOKENS * TOKENS)
    bias = jnp.dot(bias_weight.T, flat_pair, preferred_element_type=jnp.float32).reshape(HEADS, TOKENS, TOKENS)
    token_count = jnp.sum(chain_lengths)
    live_keys = jnp.arange(TOKENS, dtype=jnp.int32) < token_count

    def one_row(bias_grad, row_index):
        query_row = lax.dynamic_index_in_dim(queries, row_index, 2, keepdims=False).astype(jnp.float32)
        key_row = lax.dynamic_index_in_dim(key_vectors, row_index, 2, keepdims=False).astype(jnp.float32)
        value_row = lax.dynamic_index_in_dim(value_vectors, row_index, 2, keepdims=False).astype(jnp.float32)
        gate_row = lax.dynamic_index_in_dim(gate_logits, row_index, 2, keepdims=False).astype(jnp.float32)
        grad_row = lax.dynamic_index_in_dim(cotangent, row_index, 2, keepdims=False).astype(jnp.float32)
        scores = jnp.einsum('hdj,hdk->hjk', query_row, key_row) * score_scale + bias
        scores = jnp.where(live_keys[None, None, :], scores, -1e9)
        row_max = jnp.max(scores, axis=-1, keepdims=True)
        weights = jnp.exp(scores - row_max)
        attention = weights / jnp.sum(weights, axis=-1, keepdims=True)
        attention_b = round_bf16(attention)
        attended = jnp.einsum('hjk,hdk->hdj', attention_b, value_row)
        gate = jax.nn.sigmoid(gate_row)
        gate_grad = (grad_row * attended * gate * (1.0 - gate)).astype(jnp.bfloat16)
        attended_grad = round_bf16(grad_row * gate)
        prob_grad = jnp.einsum('hdj,hdk->hjk', attended_grad, value_row)
        row_delta = jnp.sum(attended_grad * attended, axis=1)
        score_grad = attention * (prob_grad - row_delta[:, :, None])
        score_grad_b = round_bf16(score_grad)
        query_grad = (jnp.einsum('hjk,hdk->hdj', score_grad_b, key_row) * score_scale).astype(jnp.bfloat16)
        key_grad = (jnp.einsum('hjk,hdj->hdk', score_grad_b, query_row) * score_scale).astype(jnp.bfloat16)
        value_grad = jnp.einsum('hjk,hdj->hdk', attention_b, attended_grad).astype(jnp.bfloat16)
        return bias_grad + score_grad, (query_grad, key_grad, value_grad, gate_grad)

    start_grad = jnp.zeros((HEADS, TOKENS, TOKENS), jnp.float32)
    bias_grad, stacked = lax.scan(one_row, start_grad, jnp.arange(ROWS, dtype=jnp.int32))
    query_grad, key_grad, value_grad, gate_grad = [jnp.moveaxis(item, 0, 2) for item in stacked]
    pair_grad = jnp.dot(bias_weight.astype(jnp.float32), bias_grad.reshape(HEADS, TOKENS * TOKENS), precision=lax.Precision.HIGHEST)
    pair_grad = pair_grad.reshape(PAIR, TOKENS, TOKENS).astype(jnp.bfloat16)
    return (query_grad, key_grad, value_grad, gate_grad, pair_grad)
```

```python
import functools

import jax
import jax.numpy as jnp
from jax import lax
from jax.experimental import pallas as pl
from jax.experimental.pallas import tpu as pltpu
from jax.sharding import PartitionSpec as P

HEADS = 4
HEAD_DIM = 32
TOKENS = 1024
SCALE = HEAD_DIM ** (-0.5)
LOG2E = 1.4426950408889634
KEY_BLOCK = 256
CHUNK_ROWS = 10
NEG = -1000000000.0


def contract(left, right, left_dim, right_dim):
    return lax.dot_general(
        left, right, (((left_dim,), (right_dim,)), ((), ())), preferred_element_type=jnp.float32
    )


def attention_kernel(
    count_ref, q_ref, kv_ref, gate_ref, cot_ref, bias_ref, start_ref,
    dq_ref, dgate_ref, dkv_ref, grad_ref, s_ref,
):
    cols, _, _, width = kv_ref.shape
    tokens = cols * width
    blocks = tokens // KEY_BLOCK
    per_block = KEY_BLOCK // width
    d = HEAD_DIM

    @pl.when(pl.program_id(0) == 0)
    def _():
        grad_ref[...] = start_ref[...]

    def load(block, low):
        parts = [kv_ref[block * per_block + n, 0, low:low + d, :] for n in range(per_block)]
        return parts[0] if per_block == 1 else jnp.concatenate(parts, axis=1)

    def store(block, low, value):
        for n in range(per_block):
            piece = value[:, n * width:(n + 1) * width]
            dkv_ref[block * per_block + n, 0, low:low + d, :] = piece.astype(jnp.bfloat16)

    def variant(live_blocks):
        q = q_ref[0]
        top = None
        for b in range(live_blocks):
            rows = pl.ds(b * KEY_BLOCK, KEY_BLOCK)
            s = contract(load(b, 0), q, 0, 0) * (SCALE * LOG2E) + bias_ref[rows, :]
            s_ref[rows, :] = s
            block_top = jnp.max(s, axis=0, keepdims=True)
            top = block_top if top is None else jnp.maximum(top, block_top)
        total = jnp.zeros_like(top)
        for b in range(live_blocks):
            rows = pl.ds(b * KEY_BLOCK, KEY_BLOCK)
            p = jnp.exp2(s_ref[rows, :] - top)
            s_ref[rows, :] = p
            total = total + jnp.sum(p, axis=0, keepdims=True)
        inverse = 1.0 / total
        gate = 1.0 / (1.0 + jnp.exp(-gate_ref[0].astype(jnp.float32)))
        cot = cot_ref[0].astype(jnp.float32)
        out_grad = (cot * gate).astype(jnp.bfloat16)
        attended = jnp.zeros(q.shape, jnp.float32)
        for b in range(live_blocks):
            rows = pl.ds(b * KEY_BLOCK, KEY_BLOCK)
            p = s_ref[rows, :] * inverse
            s_ref[rows, :] = p
            pb = p.astype(jnp.bfloat16)
            attended = attended + contract(load(b, d), pb, 1, 0)
            store(b, d, contract(out_grad, pb, 1, 1))
        dgate_ref[0] = (cot * attended * gate * (1.0 - gate)).astype(jnp.bfloat16)
        delta = jnp.sum(out_grad.astype(jnp.float32) * attended, axis=0, keepdims=True)
        dq = jnp.zeros(q.shape, jnp.float32)
        for b in range(live_blocks):
            rows = pl.ds(b * KEY_BLOCK, KEY_BLOCK)
            dp = contract(load(b, d), out_grad, 0, 0)
            ds = s_ref[rows, :] * (dp - delta)
            grad_ref[rows, :] = grad_ref[rows, :] + ds
            dsb = ds.astype(jnp.bfloat16)
            dq = dq + contract(load(b, 0), dsb, 1, 0)
            store(b, 0, contract(q, dsb, 1, 1) * SCALE)
        dq_ref[0] = (dq * SCALE).astype(jnp.bfloat16)
        for b in range(live_blocks, blocks):
            dead = jnp.zeros((d, KEY_BLOCK), jnp.float32)
            store(b, 0, dead)
            store(b, d, dead)

    count = count_ref[0]
    for live in range(1, blocks + 1):
        low = (live - 1) * KEY_BLOCK
        high = live * KEY_BLOCK

        @pl.when((count > low) & (count <= high))
        def _(live=live):
            variant(live)


def attention_chunk(count, q, kv, gate, cot, bias, start):
    rows, d, width = q.shape
    cols = kv.shape[0]
    kv_width = kv.shape[3]
    tokens = cols * kv_width
    row_spec = pl.BlockSpec((1, d, width), lambda i: (i, 0, 0))
    kv_spec = pl.BlockSpec((cols, 1, 2 * d, kv_width), lambda i: (0, i, 0, 0))
    square_spec = pl.BlockSpec((tokens, width), lambda i: (0, 0))
    small = jax.ShapeDtypeStruct(q.shape, jnp.bfloat16)
    return pl.pallas_call(
        attention_kernel,
        grid=(rows,),
        in_specs=[
            pl.BlockSpec(memory_space=pltpu.SMEM),
            row_spec, kv_spec, row_spec, row_spec, square_spec, square_spec,
        ],
        out_specs=[row_spec, row_spec, kv_spec, square_spec],
        out_shape=[
            small, small,
            jax.ShapeDtypeStruct(kv.shape, jnp.bfloat16),
            jax.ShapeDtypeStruct((tokens, width), jnp.float32),
        ],
        scratch_shapes=[pltpu.VMEM((tokens, width), jnp.float32)],
        compiler_params=pltpu.CompilerParams(vmem_limit_bytes=40 * 1024 * 1024),
        cost_estimate=pl.CostEstimate(
            flops=12 * rows * d * tokens * width,
            bytes_accessed=4 * rows * d * (2 * tokens + 2 * width) + 12 * tokens * width,
            transcendentals=rows * tokens * width,
        ),
    )(count, q, kv, gate, cot, bias, start)


def body(
    queries,
    key_vectors,
    value_vectors,
    gate_logits,
    cotangent,
    pair_normed,
    bias_weight,
    chain_lengths,
):
    rows_here = queries.shape[2]
    width = queries.shape[3]
    channels_here, row_block, col_block = pair_normed.shape
    col_count = lax.axis_size("col")
    count = jnp.sum(chain_lengths).reshape(1)

    def rows_first(source):
        return source[0].transpose(1, 0, 2)

    kv = jnp.concatenate([rows_first(key_vectors), rows_first(value_vectors)], axis=1)
    starts = list(range(0, rows_here, CHUNK_ROWS))
    gathered = [
        lax.all_gather(kv[a:a + CHUNK_ROWS], "col", axis=0, tiled=False) for a in starts
    ]

    flat_pair = pair_normed.reshape(channels_here, row_block * col_block)
    partial = jnp.dot(bias_weight.T, flat_pair, preferred_element_type=jnp.float32)
    partial = partial.astype(jnp.float16).reshape(HEADS, row_block, col_block)
    parts = lax.all_to_all(partial, "head", split_axis=0, concat_axis=0, tiled=True)
    own_bias = jnp.sum(parts.astype(jnp.float32), axis=0).astype(jnp.float16)
    tall = lax.all_gather(own_bias, "row", axis=0, tiled=True)
    wide = lax.all_to_all(tall, "col", split_axis=0, concat_axis=1, tiled=True)
    live = jnp.arange(TOKENS, dtype=jnp.int32)[:, None] < count[0]
    bias = jnp.where(live, wide.T.astype(jnp.float32) * LOG2E, NEG)

    q, gate, cot = rows_first(queries), rows_first(gate_logits), rows_first(cotangent)
    total = jnp.zeros((TOKENS, width), jnp.float32)
    dq, dgate, dkv = [], [], []
    for a, keys in zip(starts, gathered):
        part = slice(a, a + CHUNK_ROWS)
        dq_part, dgate_part, dkv_part, total = attention_chunk(
            count, q[part], keys, gate[part], cot[part], bias, total
        )
        dq.append(dq_part)
        dgate.append(dgate_part)
        dkv.append(lax.psum_scatter(dkv_part, "col", scatter_dimension=0, tiled=False))

    def rows_last(parts):
        return jnp.concatenate(parts, axis=0).transpose(1, 0, 2)[None]

    query_grad, gate_grad = rows_last(dq), rows_last(dgate)
    both = jnp.concatenate(dkv, axis=0).transpose(1, 0, 2)
    key_grad, value_grad = both[None, :HEAD_DIM], both[None, HEAD_DIM:]

    square = total.astype(jnp.bfloat16).T
    tall_grad = lax.all_to_all(square, "col", split_axis=1, concat_axis=0, tiled=True)
    own_grad = lax.psum_scatter(tall_grad, "row", scatter_dimension=0, tiled=True)
    every_head = lax.all_gather(own_grad, "head", axis=0, tiled=False)
    pair_grad = jnp.dot(
        bias_weight,
        every_head.reshape(HEADS, row_block * col_block),
        preferred_element_type=jnp.float32,
    )
    pair_grad = pair_grad.reshape(channels_here, row_block, col_block).astype(jnp.bfloat16)
    return (query_grad, key_grad, value_grad, gate_grad, pair_grad)


def solution(mesh):
    in_specs = (
        P("head", None, "row", "col"),
        P("head", None, "row", "col"),
        P("head", None, "row", "col"),
        P("head", None, "row", "col"),
        P("head", None, "row", "col"),
        P("head", "row", "col"),
        P("head", None),
        P(),
    )
    out_specs = (
        P("head", None, "row", "col"),
        P("head", None, "row", "col"),
        P("head", None, "row", "col"),
        P("head", None, "row", "col"),
        P("head", "row", "col"),
    )
    return jax.shard_map(body, mesh=mesh, in_specs=in_specs, out_specs=out_specs, check_vma=False)
```

```python
import functools

import jax
import jax.numpy as jnp
from jax import lax
from jax.experimental import pallas as pl
from jax.experimental.pallas import tpu as pltpu
from jax.sharding import PartitionSpec as P

HEADS = 4
HEAD_DIM = 32
TOKENS = 1024
SCALE = HEAD_DIM ** (-0.5)
LOG2E = 1.4426950408889634
NEG = -1000000000.0


def contract(left, right, left_dim, right_dim):
    return lax.dot_general(
        left, right, (((left_dim,), (right_dim,)), ((), ())), preferred_element_type=jnp.float32
    )


def attention_kernel(count_ref, in_ref, bias_ref, out_ref, grad_out_ref, s_ref, dk_ref, dv_ref, grad_ref):
    cols, _, _, width = in_ref.shape
    per = bias_ref.shape[3] // width
    d = HEAD_DIM
    row, col = pl.program_id(0), pl.program_id(1)
    side = col // per
    lanes = pl.ds(pl.multiple_of((col % per) * width, width), width)

    @pl.when((row == 0) & (col == 0))
    def _():
        grad_ref[...] = jnp.zeros_like(grad_ref)

    @pl.when(col == 0)
    def _():
        dk_ref[...] = jnp.zeros_like(dk_ref)
        dv_ref[...] = jnp.zeros_like(dv_ref)

    def key(b):
        return in_ref[b, 0, d:2 * d, :]

    def value(b):
        return in_ref[b, 0, 2 * d:3 * d, :]

    def variant(live_blocks):
        q = in_ref[col, 0, 0:d, :]
        out_grad = in_ref[col, 0, 3 * d:4 * d, :]
        top = None
        for b in range(live_blocks):
            s = contract(key(b), q, 0, 0) * (SCALE * LOG2E) + bias_ref[side, b, :, lanes]
            s_ref[b] = s
            block_top = jnp.max(s, axis=0, keepdims=True)
            top = block_top if top is None else jnp.maximum(top, block_top)
        total = jnp.zeros_like(top)
        for b in range(live_blocks):
            p = jnp.exp2(s_ref[b] - top)
            s_ref[b] = p
            total = total + jnp.sum(p, axis=0, keepdims=True)
        inverse = 1.0 / total
        attended = jnp.zeros(q.shape, jnp.float32)
        for b in range(live_blocks):
            p = s_ref[b] * inverse
            s_ref[b] = p
            pb = p.astype(jnp.bfloat16)
            attended = attended + contract(value(b), pb, 1, 0)
            dv_ref[b] += contract(out_grad, pb, 1, 1)
        out_ref[col, 0, 3 * d:4 * d, :] = attended.astype(jnp.bfloat16)
        delta = jnp.sum(out_grad.astype(jnp.float32) * attended, axis=0, keepdims=True)
        dq = jnp.zeros(q.shape, jnp.float32)
        for b in range(live_blocks):
            dp = contract(value(b), out_grad, 0, 0)
            ds = s_ref[b] * (dp - delta)
            grad_ref[side, b, :, lanes] += ds
            dsb = ds.astype(jnp.bfloat16)
            dq = dq + contract(key(b), dsb, 1, 0)
            dk_ref[b] += contract(q, dsb, 1, 1)
        out_ref[col, 0, 0:d, :] = (dq * SCALE).astype(jnp.bfloat16)

    count = count_ref[0]
    for live in range(1, cols + 1):

        @pl.when((count > (live - 1) * width) & (count <= live * width))
        def _(live=live):
            variant(live)

    @pl.when(col == cols - 1)
    def _():
        for b in range(cols):
            out_ref[b, 0, d:2 * d, :] = (dk_ref[b] * SCALE).astype(jnp.bfloat16)
            out_ref[b, 0, 2 * d:3 * d, :] = dv_ref[b].astype(jnp.bfloat16)

    @pl.when((col == cols - 1) & (row == pl.num_programs(0) - 1))
    def _():
        grad_out_ref[...] = grad_ref[...].astype(jnp.bfloat16)


def attention_rows(count, packed, bias):
    cols, rows, depth, width = packed.shape
    d = HEAD_DIM
    tokens = cols * width
    packed_spec = pl.BlockSpec((cols, 1, depth, width), lambda i, j: (0, i, 0, 0))
    bias_spec = pl.BlockSpec(bias.shape, lambda i, j: (0, 0, 0, 0))
    return pl.pallas_call(
        attention_kernel,
        grid=(rows, cols),
        in_specs=[pl.BlockSpec(memory_space=pltpu.SMEM), packed_spec, bias_spec],
        out_specs=[packed_spec, bias_spec],
        out_shape=[
            jax.ShapeDtypeStruct(packed.shape, jnp.bfloat16),
            jax.ShapeDtypeStruct(bias.shape, jnp.bfloat16),
        ],
        scratch_shapes=[
            pltpu.VMEM((cols, width, width), jnp.float32),
            pltpu.VMEM((cols, d, width), jnp.float32),
            pltpu.VMEM((cols, d, width), jnp.float32),
            pltpu.VMEM(bias.shape, jnp.float32),
        ],
        compiler_params=pltpu.CompilerParams(vmem_limit_bytes=40 * 1024 * 1024),
        cost_estimate=pl.CostEstimate(
            flops=12 * rows * d * tokens * tokens,
            bytes_accessed=4 * packed.size + 6 * bias.size,
            transcendentals=rows * tokens * tokens,
        ),
    )(count, packed, bias)


def body(
    queries,
    key_vectors,
    value_vectors,
    gate_logits,
    cotangent,
    pair_normed,
    bias_weight,
    chain_lengths,
):
    rows_here = queries.shape[2]
    channels_here, row_block, col_block = pair_normed.shape
    row_count = lax.axis_size("row")
    col_count = lax.axis_size("col")
    count = jnp.sum(chain_lengths).reshape(1)

    flat_pair = pair_normed.reshape(channels_here, row_block * col_block)
    partial = jnp.dot(bias_weight.T, flat_pair, preferred_element_type=jnp.float32)
    partial = partial.astype(jnp.float16).reshape(HEADS, row_block, col_block)
    parts = lax.all_to_all(partial, "head", split_axis=0, concat_axis=0, tiled=True)
    own_bias = jnp.sum(parts.astype(jnp.float32), axis=0).T.astype(jnp.float16)
    whole = lax.all_gather(own_bias, ("row", "col"), axis=0, tiled=False)
    whole = whole.reshape(row_count, col_count, col_block, row_block)
    position = (
        jnp.arange(col_count, dtype=jnp.int32)[:, None] * col_block
        + jnp.arange(col_block, dtype=jnp.int32)[None, :]
    )
    live = (position < count[0])[None, :, :, None]
    bias = jnp.where(live, whole.astype(jnp.float32) * LOG2E, NEG)

    gate = jax.nn.sigmoid(gate_logits.astype(jnp.float32))
    cot = cotangent.astype(jnp.float32)
    out_grad = (cot * gate).astype(jnp.bfloat16)
    packed = jnp.concatenate(
        [item[0].transpose(1, 0, 2) for item in (queries, key_vectors, value_vectors, out_grad)],
        axis=1,
    )
    packed = packed.reshape(col_count, rows_here // col_count, 4 * HEAD_DIM, col_block)
    packed = lax.all_to_all(packed, "col", split_axis=0, concat_axis=0, tiled=True)

    grads, square = attention_rows(count, packed, bias)

    grads = lax.all_to_all(grads, "col", split_axis=0, concat_axis=0, tiled=True)
    grads = grads.reshape(rows_here, 4, HEAD_DIM, col_block).transpose(1, 2, 0, 3)
    query_grad, key_grad, value_grad = grads[0:1], grads[1:2], grads[2:3]
    attended = grads[3:4].astype(jnp.float32)
    gate_grad = (cot * attended * gate * (1.0 - gate)).astype(jnp.bfloat16)

    square = square.reshape(row_count * col_count, col_block, row_block)
    own_grad = lax.psum_scatter(square, ("row", "col"), scatter_dimension=0, tiled=False).T
    every_head = lax.all_gather(own_grad, "head", axis=0, tiled=False)
    pair_grad = jnp.dot(
        bias_weight,
        every_head.reshape(HEADS, row_block * col_block),
        preferred_element_type=jnp.float32,
    )
    pair_grad = pair_grad.reshape(channels_here, row_block, col_block).astype(jnp.bfloat16)
    return (query_grad, key_grad, value_grad, gate_grad, pair_grad)


def solution(mesh):
    in_specs = (
        P("head", None, "row", "col"),
        P("head", None, "row", "col"),
        P("head", None, "row", "col"),
        P("head", None, "row", "col"),
        P("head", None, "row", "col"),
        P("head", "row", "col"),
        P("head", None),
        P(),
    )
    out_specs = (
        P("head", None, "row", "col"),
        P("head", None, "row", "col"),
        P("head", None, "row", "col"),
        P("head", None, "row", "col"),
        P("head", "row", "col"),
    )
    return jax.shard_map(body, mesh=mesh, in_specs=in_specs, out_specs=out_specs, check_vma=False)
```

```python
import functools

import jax
import jax.numpy as jnp
from jax import lax
from jax.experimental import pallas as pl
from jax.experimental.pallas import tpu as pltpu
from jax.sharding import PartitionSpec as P

HEADS = 4
HEAD_DIM = 32
TOKENS = 1024
SCALE = HEAD_DIM ** (-0.5)
SUB = 16
ROW_TILE = 64
PAIR_HERE = 32
LOG2E = 1.4426950408889634
NEG = -1000000000.0


def contract(left, right, left_dim, right_dim):
    return lax.dot_general(
        left, right, (((left_dim,), (right_dim,)), ((), ())), preferred_element_type=jnp.float32
    )


def attention_kernel(count_ref, in_ref, bias_ref, out_ref, grad_out_ref, s_ref, dk_ref, dv_ref, grad_ref):
    cols, _, _, width = in_ref.shape
    per = bias_ref.shape[3] // width
    d = HEAD_DIM
    row, col = pl.program_id(0), pl.program_id(1)
    side = col // per
    lanes = pl.ds(pl.multiple_of((col % per) * width, width), width)

    @pl.when((row == 0) & (col == 0))
    def _():
        grad_ref[...] = jnp.zeros_like(grad_ref)

    @pl.when(col == 0)
    def _():
        dk_ref[...] = jnp.zeros_like(dk_ref)
        dv_ref[...] = jnp.zeros_like(dv_ref)

    def key(b):
        return in_ref[b, 0, d:2 * d, :]

    def value(b):
        return in_ref[b, 0, 2 * d:3 * d, :]

    def variant(live_blocks):
        q = in_ref[col, 0, 0:d, :]
        out_grad = in_ref[col, 0, 3 * d:4 * d, :]
        top = None
        for b in range(live_blocks):
            s = contract(key(b), q, 0, 0) * (SCALE * LOG2E) + bias_ref[side, b, :, lanes]
            s_ref[b] = s
            block_top = jnp.max(s, axis=0, keepdims=True)
            top = block_top if top is None else jnp.maximum(top, block_top)
        total = jnp.zeros_like(top)
        for b in range(live_blocks):
            p = jnp.exp2(s_ref[b] - top)
            s_ref[b] = p
            total = total + jnp.sum(p, axis=0, keepdims=True)
        inverse = 1.0 / total
        attended = jnp.zeros(q.shape, jnp.float32)
        for b in range(live_blocks):
            p = s_ref[b] * inverse
            s_ref[b] = p
            pb = p.astype(jnp.bfloat16)
            attended = attended + contract(value(b), pb, 1, 0)
            dv_ref[b] += contract(out_grad, pb, 1, 1)
        out_ref[col, 0, 3 * d:4 * d, :] = attended.astype(jnp.bfloat16)
        delta = jnp.sum(out_grad.astype(jnp.float32) * attended, axis=0, keepdims=True)
        dq = jnp.zeros(q.shape, jnp.float32)
        for b in range(live_blocks):
            dp = contract(value(b), out_grad, 0, 0)
            ds = s_ref[b] * (dp - delta)
            grad_ref[side, b, :, lanes] += ds
            dsb = ds.astype(jnp.bfloat16)
            dq = dq + contract(key(b), dsb, 1, 0)
            dk_ref[b] += contract(q, dsb, 1, 1)
        out_ref[col, 0, 0:d, :] = (dq * SCALE).astype(jnp.bfloat16)

    count = count_ref[0]
    for live in range(1, cols + 1):

        @pl.when((count > (live - 1) * width) & (count <= live * width))
        def _(live=live):
            variant(live)

    @pl.when(col == cols - 1)
    def _():
        for b in range(cols):
            out_ref[b, 0, d:2 * d, :] = (dk_ref[b] * SCALE).astype(jnp.bfloat16)
            out_ref[b, 0, 2 * d:3 * d, :] = dv_ref[b].astype(jnp.bfloat16)

    @pl.when((col == cols - 1) & (row == pl.num_programs(0) - 1))
    def _():
        grad_out_ref[...] = grad_ref[...].astype(jnp.bfloat16)


def attention_rows(count, packed, bias):
    cols, rows, depth, width = packed.shape
    d = HEAD_DIM
    tokens = cols * width
    packed_spec = pl.BlockSpec((cols, 1, depth, width), lambda i, j: (0, i, 0, 0))
    bias_spec = pl.BlockSpec(bias.shape, lambda i, j: (0, 0, 0, 0))
    return pl.pallas_call(
        attention_kernel,
        grid=(rows, cols),
        in_specs=[pl.BlockSpec(memory_space=pltpu.SMEM), packed_spec, bias_spec],
        out_specs=[packed_spec, bias_spec],
        out_shape=[
            jax.ShapeDtypeStruct(packed.shape, jnp.bfloat16),
            jax.ShapeDtypeStruct(bias.shape, jnp.bfloat16),
        ],
        scratch_shapes=[
            pltpu.VMEM((cols, width, width), jnp.float32),
            pltpu.VMEM((cols, d, width), jnp.float32),
            pltpu.VMEM((cols, d, width), jnp.float32),
            pltpu.VMEM(bias.shape, jnp.float32),
        ],
        compiler_params=pltpu.CompilerParams(vmem_limit_bytes=40 * 1024 * 1024),
        cost_estimate=pl.CostEstimate(
            flops=12 * rows * d * tokens * tokens,
            bytes_accessed=4 * packed.size + 6 * bias.size,
            transcendentals=rows * tokens * tokens,
        ),
    )(count, packed, bias)


def project_kernel(weight_ref, pair_ref, out_ref):
    channels, rows, _ = pair_ref.shape

    def step(i, carry):
        part = pl.ds(pl.multiple_of(i * SUB, SUB), SUB)
        sums = [None] * HEADS
        for c in range(channels):
            x = pair_ref[c, part, :].astype(jnp.float32)
            for h in range(HEADS):
                term = x * weight_ref[c * HEADS + h]
                sums[h] = term if sums[h] is None else sums[h] + term
        for h in range(HEADS):
            out_ref[h, part, :] = sums[h]
        return carry

    lax.fori_loop(0, rows // SUB, step, 0)


def expand_kernel(weight_ref, grad_ref, out_ref):
    channels, rows, _ = out_ref.shape

    def step(i, carry):
        part = pl.ds(pl.multiple_of(i * SUB, SUB), SUB)
        heads = [grad_ref[h, part, :].astype(jnp.float32) for h in range(HEADS)]
        for c in range(channels):
            total = heads[0] * weight_ref[c * HEADS]
            for h in range(1, HEADS):
                total = total + heads[h] * weight_ref[c * HEADS + h]
            out_ref[c, part, :] = total.astype(jnp.bfloat16)
        return carry

    lax.fori_loop(0, rows // SUB, step, 0)


def pair_call(kernel, weight, source, leading, dtype):
    _, rows, width = source.shape
    tile = min(ROW_TILE, rows)
    return pl.pallas_call(
        kernel,
        grid=(rows // tile,),
        in_specs=[
            pl.BlockSpec(memory_space=pltpu.SMEM),
            pl.BlockSpec((source.shape[0], tile, width), lambda i: (0, i, 0)),
        ],
        out_specs=pl.BlockSpec((leading, tile, width), lambda i: (0, i, 0)),
        out_shape=jax.ShapeDtypeStruct((leading, rows, width), dtype),
        compiler_params=pltpu.CompilerParams(vmem_limit_bytes=40 * 1024 * 1024),
        cost_estimate=pl.CostEstimate(
            flops=2 * HEADS * PAIR_HERE * rows * width,
            bytes_accessed=(2 * PAIR_HERE + 4 * HEADS) * rows * width,
            transcendentals=0,
        ),
    )(weight, source)


def body(
    queries,
    key_vectors,
    value_vectors,
    gate_logits,
    cotangent,
    pair_normed,
    bias_weight,
    chain_lengths,
):
    rows_here = queries.shape[2]
    channels_here, row_block, col_block = pair_normed.shape
    row_count = lax.axis_size("row")
    col_count = lax.axis_size("col")
    count = jnp.sum(chain_lengths).reshape(1)

    weight = bias_weight.astype(jnp.float32).reshape(-1)
    partial = pair_call(project_kernel, weight, pair_normed, HEADS, jnp.float32)
    partial = partial.astype(jnp.float16)
    parts = lax.all_to_all(partial, "head", split_axis=0, concat_axis=0, tiled=True)
    own_bias = jnp.sum(parts.astype(jnp.float32), axis=0).T.astype(jnp.float16)
    line = lax.all_gather(own_bias, "col", axis=0, tiled=True)
    whole = lax.all_gather(line, "row", axis=0, tiled=True)
    whole = whole.reshape(row_count, col_count, col_block, row_block)
    position = (
        jnp.arange(col_count, dtype=jnp.int32)[:, None] * col_block
        + jnp.arange(col_block, dtype=jnp.int32)[None, :]
    )
    live = (position < count[0])[None, :, :, None]
    bias = jnp.where(live, whole.astype(jnp.float32) * LOG2E, NEG)

    gate = jax.nn.sigmoid(gate_logits.astype(jnp.float32))
    cot = cotangent.astype(jnp.float32)
    out_grad = (cot * gate).astype(jnp.bfloat16)
    packed = jnp.concatenate(
        [item[0].transpose(1, 0, 2) for item in (queries, key_vectors, value_vectors, out_grad)],
        axis=1,
    )
    packed = packed.reshape(col_count, rows_here // col_count, 4 * HEAD_DIM, col_block)
    packed = lax.all_to_all(packed, "col", split_axis=0, concat_axis=0, tiled=True)

    grads, square = attention_rows(count, packed, bias)

    grads = lax.all_to_all(grads, "col", split_axis=0, concat_axis=0, tiled=True)
    grads = grads.reshape(rows_here, 4, HEAD_DIM, col_block).transpose(1, 2, 0, 3)
    query_grad, key_grad, value_grad = grads[0:1], grads[1:2], grads[2:3]
    attended = grads[3:4].astype(jnp.float32)
    gate_grad = (cot * attended * gate * (1.0 - gate)).astype(jnp.bfloat16)

    square = square.reshape(row_count * col_count * col_block, row_block)
    line_grad = lax.psum_scatter(square, "row", scatter_dimension=0, tiled=True)
    own_grad = lax.psum_scatter(line_grad, "col", scatter_dimension=0, tiled=True).T
    every_head = lax.all_gather(own_grad, "head", axis=0, tiled=False)
    pair_grad = pair_call(expand_kernel, weight, every_head, channels_here, jnp.bfloat16)
    return (query_grad, key_grad, value_grad, gate_grad, pair_grad)


def solution(mesh):
    in_specs = (
        P("head", None, "row", "col"),
        P("head", None, "row", "col"),
        P("head", None, "row", "col"),
        P("head", None, "row", "col"),
        P("head", None, "row", "col"),
        P("head", "row", "col"),
        P("head", None),
        P(),
    )
    out_specs = (
        P("head", None, "row", "col"),
        P("head", None, "row", "col"),
        P("head", None, "row", "col"),
        P("head", None, "row", "col"),
        P("head", "row", "col"),
    )
    return jax.shard_map(body, mesh=mesh, in_specs=in_specs, out_specs=out_specs, check_vma=False)
```

```python
import functools

import jax
import jax.numpy as jnp
from jax import lax
from jax.experimental import pallas as pl
from jax.experimental.pallas import tpu as pltpu
from jax.sharding import PartitionSpec as P

HEADS = 4
HEAD_DIM = 32
TOKENS = 1024
SCALE = HEAD_DIM ** (-0.5)
SUB = 16
ROW_TILE = 64
PAIR_HERE = 32
LOG2E = 1.4426950408889634
NEG = -1000000000.0


def contract(left, right, left_dim, right_dim):
    return lax.dot_general(
        left, right, (((left_dim,), (right_dim,)), ((), ())), preferred_element_type=jnp.float32
    )


def attention_kernel(count_ref, qk_ref, va_ref, bias_ref, out_ref, grad_out_ref, s_ref, dk_ref, dv_ref, grad_ref):
    cols, _, _, width = qk_ref.shape
    per = bias_ref.shape[3] // width
    d = HEAD_DIM
    row, col = pl.program_id(0), pl.program_id(1)
    side = col // per
    lanes = pl.ds(pl.multiple_of((col % per) * width, width), width)

    @pl.when((row == 0) & (col == 0))
    def _():
        grad_ref[...] = jnp.zeros_like(grad_ref)

    @pl.when(col == 0)
    def _():
        dk_ref[...] = jnp.zeros_like(dk_ref)
        dv_ref[...] = jnp.zeros_like(dv_ref)

    def key(b):
        return qk_ref[b, 0, d:2 * d, :]

    def value(b):
        return va_ref[b, 0, 0:d, :]

    def variant(live_blocks):
        q = qk_ref[col, 0, 0:d, :]
        out_grad = va_ref[col, 0, d:2 * d, :]
        top = None
        for b in range(live_blocks):
            s = contract(key(b), q, 0, 0) * (SCALE * LOG2E) + bias_ref[side, b, :, lanes]
            s_ref[b] = s
            block_top = jnp.max(s, axis=0, keepdims=True)
            top = block_top if top is None else jnp.maximum(top, block_top)
        total = jnp.zeros_like(top)
        for b in range(live_blocks):
            p = jnp.exp2(s_ref[b] - top)
            s_ref[b] = p
            total = total + jnp.sum(p, axis=0, keepdims=True)
        inverse = 1.0 / total
        attended = jnp.zeros(q.shape, jnp.float32)
        for b in range(live_blocks):
            p = s_ref[b] * inverse
            s_ref[b] = p
            pb = p.astype(jnp.bfloat16)
            attended = attended + contract(value(b), pb, 1, 0)
            dv_ref[b] += contract(out_grad, pb, 1, 1)
        out_ref[col, 0, 3 * d:4 * d, :] = attended.astype(jnp.bfloat16)
        delta = jnp.sum(out_grad.astype(jnp.float32) * attended, axis=0, keepdims=True)
        dq = jnp.zeros(q.shape, jnp.float32)
        for b in range(live_blocks):
            dp = contract(value(b), out_grad, 0, 0)
            ds = s_ref[b] * (dp - delta)
            grad_ref[side, b, :, lanes] += ds
            dsb = ds.astype(jnp.bfloat16)
            dq = dq + contract(key(b), dsb, 1, 0)
            dk_ref[b] += contract(q, dsb, 1, 1)
        out_ref[col, 0, 0:d, :] = (dq * SCALE).astype(jnp.bfloat16)

    count = count_ref[0]
    for live in range(1, cols + 1):

        @pl.when((count > (live - 1) * width) & (count <= live * width))
        def _(live=live):
            variant(live)

    @pl.when(col == cols - 1)
    def _():
        for b in range(cols):
            out_ref[b, 0, d:2 * d, :] = (dk_ref[b] * SCALE).astype(jnp.bfloat16)
            out_ref[b, 0, 2 * d:3 * d, :] = dv_ref[b].astype(jnp.bfloat16)

    @pl.when((col == cols - 1) & (row == pl.num_programs(0) - 1))
    def _():
        grad_out_ref[...] = grad_ref[...].astype(jnp.bfloat16)


def attention_rows(count, qk, va, bias):
    cols, rows, depth, width = qk.shape
    d = HEAD_DIM
    tokens = cols * width
    half_spec = pl.BlockSpec((cols, 1, depth, width), lambda i, j: (0, i, 0, 0))
    packed_spec = pl.BlockSpec((cols, 1, 2 * depth, width), lambda i, j: (0, i, 0, 0))
    bias_spec = pl.BlockSpec(bias.shape, lambda i, j: (0, 0, 0, 0))
    return pl.pallas_call(
        attention_kernel,
        grid=(rows, cols),
        in_specs=[pl.BlockSpec(memory_space=pltpu.SMEM), half_spec, half_spec, bias_spec],
        out_specs=[packed_spec, bias_spec],
        out_shape=[
            jax.ShapeDtypeStruct((cols, rows, 2 * depth, width), jnp.bfloat16),
            jax.ShapeDtypeStruct(bias.shape, jnp.bfloat16),
        ],
        scratch_shapes=[
            pltpu.VMEM((cols, width, width), jnp.float32),
            pltpu.VMEM((cols, d, width), jnp.float32),
            pltpu.VMEM((cols, d, width), jnp.float32),
            pltpu.VMEM(bias.shape, jnp.float32),
        ],
        compiler_params=pltpu.CompilerParams(vmem_limit_bytes=40 * 1024 * 1024),
        cost_estimate=pl.CostEstimate(
            flops=12 * rows * d * tokens * tokens,
            bytes_accessed=8 * qk.size + 6 * bias.size,
            transcendentals=rows * tokens * tokens,
        ),
    )(count, qk, va, bias)


def project_kernel(weight_ref, pair_ref, out_ref):
    channels, rows, _ = pair_ref.shape

    def step(i, carry):
        part = pl.ds(pl.multiple_of(i * SUB, SUB), SUB)
        sums = [None] * HEADS
        for c in range(channels):
            x = pair_ref[c, part, :].astype(jnp.float32)
            for h in range(HEADS):
                term = x * weight_ref[c * HEADS + h]
                sums[h] = term if sums[h] is None else sums[h] + term
        for h in range(HEADS):
            out_ref[h, part, :] = sums[h]
        return carry

    lax.fori_loop(0, rows // SUB, step, 0)


def expand_kernel(weight_ref, grad_ref, out_ref):
    channels, rows, _ = out_ref.shape

    def step(i, carry):
        part = pl.ds(pl.multiple_of(i * SUB, SUB), SUB)
        heads = [grad_ref[h, part, :].astype(jnp.float32) for h in range(HEADS)]
        for c in range(channels):
            total = heads[0] * weight_ref[c * HEADS]
            for h in range(1, HEADS):
                total = total + heads[h] * weight_ref[c * HEADS + h]
            out_ref[c, part, :] = total.astype(jnp.bfloat16)
        return carry

    lax.fori_loop(0, rows // SUB, step, 0)


def pair_call(kernel, weight, source, leading, dtype):
    _, rows, width = source.shape
    tile = min(ROW_TILE, rows)
    return pl.pallas_call(
        kernel,
        grid=(rows // tile,),
        in_specs=[
            pl.BlockSpec(memory_space=pltpu.SMEM),
            pl.BlockSpec((source.shape[0], tile, width), lambda i: (0, i, 0)),
        ],
        out_specs=pl.BlockSpec((leading, tile, width), lambda i: (0, i, 0)),
        out_shape=jax.ShapeDtypeStruct((leading, rows, width), dtype),
        compiler_params=pltpu.CompilerParams(vmem_limit_bytes=40 * 1024 * 1024),
        cost_estimate=pl.CostEstimate(
            flops=2 * HEADS * PAIR_HERE * rows * width,
            bytes_accessed=(2 * PAIR_HERE + 4 * HEADS) * rows * width,
            transcendentals=0,
        ),
    )(weight, source)


def body(
    queries,
    key_vectors,
    value_vectors,
    gate_logits,
    cotangent,
    pair_normed,
    bias_weight,
    chain_lengths,
):
    rows_here = queries.shape[2]
    channels_here, row_block, col_block = pair_normed.shape
    row_count = lax.axis_size("row")
    col_count = lax.axis_size("col")
    count = jnp.sum(chain_lengths).reshape(1)

    def pack(items):
        packed = jnp.concatenate([item[0].transpose(1, 0, 2) for item in items], axis=1)
        return packed.reshape(col_count, rows_here // col_count, 2 * HEAD_DIM, col_block)

    def exchange(packed):
        return lax.all_to_all(packed, "col", split_axis=0, concat_axis=0, tiled=True)

    gate = jax.nn.sigmoid(gate_logits.astype(jnp.float32))
    cot = cotangent.astype(jnp.float32)
    qk = pack((queries, key_vectors))
    qk, pair_normed = lax.optimization_barrier((qk, pair_normed))
    qk = exchange(qk)

    weight = bias_weight.astype(jnp.float32).reshape(-1)
    partial = pair_call(project_kernel, weight, pair_normed, HEADS, jnp.float32)
    partial = partial.astype(jnp.float16)
    head_count = lax.axis_size("head")
    head = lax.axis_index("head")
    own_bias = lax.dynamic_index_in_dim(partial, head, 0, keepdims=False).astype(jnp.float32)
    for shift in range(1, head_count):
        sent = lax.dynamic_index_in_dim(partial, (head + shift) % head_count, 0, keepdims=False)
        perm = [(i, (i + shift) % head_count) for i in range(head_count)]
        own_bias = own_bias + lax.ppermute(sent, "head", perm).astype(jnp.float32)
    own_bias = own_bias.T.astype(jnp.float16)
    va = pack((value_vectors, (cot * gate).astype(jnp.bfloat16)))
    own_bias, qk, va = lax.optimization_barrier((own_bias, qk, va))
    va = exchange(va)
    line = lax.all_gather(own_bias, "col", axis=0, tiled=True)
    whole = lax.all_gather(line, "row", axis=0, tiled=True)
    whole = whole.reshape(row_count, col_count, col_block, row_block)
    position = (
        jnp.arange(col_count, dtype=jnp.int32)[:, None] * col_block
        + jnp.arange(col_block, dtype=jnp.int32)[None, :]
    )
    live = (position < count[0])[None, :, :, None]
    bias = jnp.where(live, whole.astype(jnp.float32) * LOG2E, NEG)

    grads, square = attention_rows(count, qk, va, bias)

    grads = lax.all_to_all(grads, "col", split_axis=0, concat_axis=0, tiled=True)
    grads = grads.reshape(rows_here, 4, HEAD_DIM, col_block).transpose(1, 2, 0, 3)
    query_grad, key_grad, value_grad = grads[0:1], grads[1:2], grads[2:3]
    attended = grads[3:4].astype(jnp.float32)
    gate_grad = (cot * attended * gate * (1.0 - gate)).astype(jnp.bfloat16)

    square = square.reshape(row_count * col_count * col_block, row_block)
    line_grad = lax.psum_scatter(square, "row", scatter_dimension=0, tiled=True)
    own_grad = lax.psum_scatter(line_grad, "col", scatter_dimension=0, tiled=True).T
    every_head = lax.all_gather(own_grad, "head", axis=0, tiled=False)
    pair_grad = pair_call(expand_kernel, weight, every_head, channels_here, jnp.bfloat16)
    return (query_grad, key_grad, value_grad, gate_grad, pair_grad)


def solution(mesh):
    in_specs = (
        P("head", None, "row", "col"),
        P("head", None, "row", "col"),
        P("head", None, "row", "col"),
        P("head", None, "row", "col"),
        P("head", None, "row", "col"),
        P("head", "row", "col"),
        P("head", None),
        P(),
    )
    out_specs = (
        P("head", None, "row", "col"),
        P("head", None, "row", "col"),
        P("head", None, "row", "col"),
        P("head", None, "row", "col"),
        P("head", "row", "col"),
    )
    return jax.shard_map(body, mesh=mesh, in_specs=in_specs, out_specs=out_specs, check_vma=False)
```

```python
import functools

import jax
import jax.numpy as jnp
from jax import lax
from jax.experimental import pallas as pl
from jax.experimental.layout import Layout, with_layout_constraint
from jax.experimental.pallas import tpu as pltpu
from jax.sharding import PartitionSpec as P

HEADS = 4
HEAD_DIM = 32
TOKENS = 1024
SCALE = HEAD_DIM ** (-0.5)
SUB = 16
ROW_TILE = 64
PAIR_HERE = 32
LOG2E = 1.4426950408889634
NEG = -1000000000.0


def contract(left, right, left_dim, right_dim):
    return lax.dot_general(
        left, right, (((left_dim,), (right_dim,)), ((), ())), preferred_element_type=jnp.float32
    )


def attention_kernel(count_ref, qk_ref, va_ref, bias_ref, out_ref, grad_out_ref, s_ref, dk_ref, dv_ref, grad_ref):
    cols, _, _, width = qk_ref.shape
    per = bias_ref.shape[3] // width
    d = HEAD_DIM
    row, col = pl.program_id(0), pl.program_id(1)
    side = col // per
    lanes = pl.ds(pl.multiple_of((col % per) * width, width), width)

    @pl.when((row == 0) & (col == 0))
    def _():
        grad_ref[...] = jnp.zeros_like(grad_ref)

    @pl.when(col == 0)
    def _():
        dk_ref[...] = jnp.zeros_like(dk_ref)
        dv_ref[...] = jnp.zeros_like(dv_ref)

    def key(b):
        return qk_ref[b, 0, d:2 * d, :]

    def value(b):
        return va_ref[b, 0, 0:d, :]

    def variant(live_blocks):
        q = qk_ref[col, 0, 0:d, :]
        out_grad = va_ref[col, 0, d:2 * d, :]
        scaled = q.astype(jnp.float32) * (SCALE * LOG2E)
        high = scaled.astype(jnp.bfloat16)
        low = (scaled - high.astype(jnp.float32)).astype(jnp.bfloat16)
        pair = jnp.concatenate([high, low], axis=0)
        top = None
        for b in range(live_blocks):
            twice = jnp.concatenate([key(b), key(b)], axis=0)
            s = contract(twice, pair, 0, 0) + bias_ref[b, side, :, lanes]
            s_ref[b] = s
            block_top = jnp.max(s, axis=0, keepdims=True)
            top = block_top if top is None else jnp.maximum(top, block_top)
        total = jnp.zeros_like(top)
        for b in range(live_blocks):
            p = jnp.exp2(s_ref[b] - top)
            s_ref[b] = p
            total = total + jnp.sum(p, axis=0, keepdims=True)
        inverse = 1.0 / total
        attended = jnp.zeros(q.shape, jnp.float32)
        for b in range(live_blocks):
            p = s_ref[b] * inverse
            s_ref[b] = p
            pb = p.astype(jnp.bfloat16)
            attended = attended + contract(value(b), pb, 1, 0)
            dv_ref[b] += contract(out_grad, pb, 1, 1)
        out_ref[col, 0, 3 * d:4 * d, :] = attended.astype(jnp.bfloat16)
        delta = jnp.sum(out_grad.astype(jnp.float32) * attended, axis=0, keepdims=True)
        rest = -delta
        thirds = []
        for _ in range(3):
            third = rest.astype(jnp.bfloat16).astype(jnp.float32)
            thirds.append(third)
            rest = rest - third
        place = lax.broadcasted_iota(jnp.int32, q.shape, 0)
        extra = jnp.where(place == 0, thirds[0], jnp.where(place == 1, thirds[1], 0.0))
        extra = jnp.where(place == 2, thirds[2], extra).astype(jnp.bfloat16)
        longer = jnp.concatenate([out_grad, extra], axis=0)
        ones = jnp.ones(q.shape, jnp.bfloat16)
        dq = jnp.zeros(q.shape, jnp.float32)
        for b in range(live_blocks):
            ds = s_ref[b] * contract(jnp.concatenate([value(b), ones], axis=0), longer, 0, 0)
            grad_ref[side, b, :, lanes] += ds
            dsb = ds.astype(jnp.bfloat16)
            dq = dq + contract(key(b), dsb, 1, 0)
            dk_ref[b] += contract(q, dsb, 1, 1)
        out_ref[col, 0, 0:d, :] = (dq * SCALE).astype(jnp.bfloat16)

    count = count_ref[0]
    for live in range(1, cols + 1):

        @pl.when((count > (live - 1) * width) & (count <= live * width))
        def _(live=live):
            variant(live)

    @pl.when(col == cols - 1)
    def _():
        for b in range(cols):
            out_ref[b, 0, d:2 * d, :] = (dk_ref[b] * SCALE).astype(jnp.bfloat16)
            out_ref[b, 0, 2 * d:3 * d, :] = dv_ref[b].astype(jnp.bfloat16)

    @pl.when((col == cols - 1) & (row == pl.num_programs(0) - 1))
    def _():
        grad_out_ref[...] = grad_ref[...].astype(jnp.bfloat16)


def attention_rows(count, qk, va, bias):
    cols, rows, depth, width = qk.shape
    d = HEAD_DIM
    tokens = cols * width
    half_spec = pl.BlockSpec((cols, 1, depth, width), lambda i, j: (0, i, 0, 0))
    packed_spec = pl.BlockSpec((cols, 1, 2 * depth, width), lambda i, j: (0, i, 0, 0))
    bias_spec = pl.BlockSpec(bias.shape, lambda i, j: (0, 0, 0, 0))
    square = (bias.shape[1], bias.shape[0]) + bias.shape[2:]
    square_spec = pl.BlockSpec(square, lambda i, j: (0, 0, 0, 0))
    return pl.pallas_call(
        attention_kernel,
        grid=(rows, cols),
        in_specs=[pl.BlockSpec(memory_space=pltpu.SMEM), half_spec, half_spec, bias_spec],
        out_specs=[packed_spec, square_spec],
        out_shape=[
            jax.ShapeDtypeStruct((cols, rows, 2 * depth, width), jnp.bfloat16),
            jax.ShapeDtypeStruct(square, jnp.bfloat16),
        ],
        scratch_shapes=[
            pltpu.VMEM((cols, width, width), jnp.float32),
            pltpu.VMEM((cols, d, width), jnp.float32),
            pltpu.VMEM((cols, d, width), jnp.float32),
            pltpu.VMEM(square, jnp.float32),
        ],
        compiler_params=pltpu.CompilerParams(vmem_limit_bytes=40 * 1024 * 1024),
        cost_estimate=pl.CostEstimate(
            flops=12 * rows * d * tokens * tokens,
            bytes_accessed=8 * qk.size + 6 * bias.size,
            transcendentals=rows * tokens * tokens,
        ),
    )(count, qk, va, bias)


def project_kernel(weight_ref, pair_ref, out_ref):
    channels, rows, _ = pair_ref.shape

    def step(i, carry):
        part = pl.ds(pl.multiple_of(i * SUB, SUB), SUB)
        sums = [None] * HEADS
        for c in range(channels):
            x = pair_ref[c, part, :].astype(jnp.float32)
            for h in range(HEADS):
                term = x * weight_ref[c * HEADS + h]
                sums[h] = term if sums[h] is None else sums[h] + term
        for h in range(HEADS):
            out_ref[h, part, :] = sums[h]
        return carry

    lax.fori_loop(0, rows // SUB, step, 0)


def expand_kernel(weight_ref, grad_ref, out_ref):
    channels, rows, _ = out_ref.shape

    def step(i, carry):
        part = pl.ds(pl.multiple_of(i * SUB, SUB), SUB)
        heads = [grad_ref[h, part, :].astype(jnp.float32) for h in range(HEADS)]
        for c in range(channels):
            total = heads[0] * weight_ref[c * HEADS]
            for h in range(1, HEADS):
                total = total + heads[h] * weight_ref[c * HEADS + h]
            out_ref[c, part, :] = total.astype(jnp.bfloat16)
        return carry

    lax.fori_loop(0, rows // SUB, step, 0)


def pair_call(kernel, weight, source, leading, dtype):
    _, rows, width = source.shape
    tile = min(ROW_TILE, rows)
    return pl.pallas_call(
        kernel,
        grid=(rows // tile,),
        in_specs=[
            pl.BlockSpec(memory_space=pltpu.SMEM),
            pl.BlockSpec((source.shape[0], tile, width), lambda i: (0, i, 0)),
        ],
        out_specs=pl.BlockSpec((leading, tile, width), lambda i: (0, i, 0)),
        out_shape=jax.ShapeDtypeStruct((leading, rows, width), dtype),
        compiler_params=pltpu.CompilerParams(vmem_limit_bytes=40 * 1024 * 1024),
        cost_estimate=pl.CostEstimate(
            flops=2 * HEADS * PAIR_HERE * rows * width,
            bytes_accessed=(2 * PAIR_HERE + 4 * HEADS) * rows * width,
            transcendentals=0,
        ),
    )(weight, source)


def body(
    queries,
    key_vectors,
    value_vectors,
    gate_logits,
    cotangent,
    pair_normed,
    bias_weight,
    chain_lengths,
):
    rows_here = queries.shape[2]
    channels_here, row_block, col_block = pair_normed.shape
    row_count = lax.axis_size("row")
    col_count = lax.axis_size("col")
    count = jnp.sum(chain_lengths).reshape(1)

    def pack(items):
        packed = jnp.concatenate([item[0].transpose(1, 0, 2) for item in items], axis=1)
        return packed.reshape(col_count, rows_here // col_count, 2 * HEAD_DIM, col_block)

    def exchange(packed):
        return lax.all_to_all(packed, "col", split_axis=0, concat_axis=0, tiled=True)

    gate = jax.nn.sigmoid(gate_logits.astype(jnp.float32))
    cot = cotangent.astype(jnp.float32)
    qk = pack((queries, key_vectors))
    qk, pair_normed = lax.optimization_barrier((qk, pair_normed))
    qk = exchange(qk)

    weight = bias_weight.astype(jnp.float32).reshape(-1)
    partial = pair_call(project_kernel, weight, pair_normed, HEADS, jnp.float32)
    partial = partial.astype(jnp.float16)
    head_count = lax.axis_size("head")
    head = lax.axis_index("head")
    own_bias = lax.dynamic_index_in_dim(partial, head, 0, keepdims=False).astype(jnp.float32)
    for shift in range(1, head_count):
        sent = lax.dynamic_index_in_dim(partial, (head + shift) % head_count, 0, keepdims=False)
        perm = [(i, (i + shift) % head_count) for i in range(head_count)]
        own_bias = own_bias + lax.ppermute(sent, "head", perm).astype(jnp.float32)
    own_bias = own_bias.T.astype(jnp.float16)
    own_bias = with_layout_constraint(own_bias, Layout(major_to_minor=(0, 1)))
    va = pack((value_vectors, (cot * gate).astype(jnp.bfloat16)))
    own_bias, qk, va = lax.optimization_barrier((own_bias, qk, va))
    va = exchange(va)
    line = lax.all_gather(own_bias, "row", axis=0, tiled=True)
    whole = lax.all_gather(line, "col", axis=0, tiled=True)
    whole = with_layout_constraint(whole, Layout(major_to_minor=(0, 1)))
    whole = whole.reshape(col_count, row_count, col_block, row_block)
    position = (
        jnp.arange(col_count, dtype=jnp.int32)[:, None] * col_block
        + jnp.arange(col_block, dtype=jnp.int32)[None, :]
    )
    live = (position < count[0])[:, None, :, None]
    bias = jnp.where(live, whole.astype(jnp.float32) * LOG2E, NEG)

    grads, square = attention_rows(count, qk, va, bias)

    grads = lax.all_to_all(grads, "col", split_axis=0, concat_axis=0, tiled=True)
    grads = grads.reshape(rows_here, 4, HEAD_DIM, col_block).transpose(1, 2, 0, 3)
    query_grad, key_grad, value_grad = grads[0:1], grads[1:2], grads[2:3]
    attended = grads[3:4].astype(jnp.float32)
    gate_grad = (cot * attended * gate * (1.0 - gate)).astype(jnp.bfloat16)

    square = square.reshape(row_count * col_count * col_block, row_block)
    line_grad = lax.psum_scatter(square, "row", scatter_dimension=0, tiled=True)
    own_grad = lax.psum_scatter(line_grad, "col", scatter_dimension=0, tiled=True).T
    every_head = lax.all_gather(own_grad, "head", axis=0, tiled=False)
    pair_grad = pair_call(expand_kernel, weight, every_head, channels_here, jnp.bfloat16)
    return (query_grad, key_grad, value_grad, gate_grad, pair_grad)


def solution(mesh):
    in_specs = (
        P("head", None, "row", "col"),
        P("head", None, "row", "col"),
        P("head", None, "row", "col"),
        P("head", None, "row", "col"),
        P("head", None, "row", "col"),
        P("head", "row", "col"),
        P("head", None),
        P(),
    )
    out_specs = (
        P("head", None, "row", "col"),
        P("head", None, "row", "col"),
        P("head", None, "row", "col"),
        P("head", None, "row", "col"),
        P("head", "row", "col"),
    )
    return jax.shard_map(body, mesh=mesh, in_specs=in_specs, out_specs=out_specs, check_vma=False)
```
